32 devices in a mesh: groups: 2 (over y), block: 8 (over z, core), dp: 1, seq: 2 (over x).
Axes of the slice: x: 2, y: 2, z: 4, core: 2. Of those that a mesh axis runs over, the one named last changes fastest.
Arguments:
- inputs: float32 [4096, 2, 1024], P('block', 'groups', ('dp', 'seq')), parts along dimension 1, may hold values from -6 to 6
- cotangent: float32 [4096, 2, 1024], P('block', 'groups', ('dp', 'seq')), parts along dimension 1, may hold values from -6 to 6
- seq_right: float32 [8, 128, 128], P(('dp', 'seq')), may hold values from -0.5 to 0.5
- seq_left: float32 [128, 8, 8], P(('dp', 'seq')), may hold values from -2 to 2
- seq_gain: float32 [4096], P('block'), may hold values from 0.5 to 2
- gate_right: float32 [64, 64, 64], P('block'), may hold values from -0.75 to 0.75
- gate_left: float32 [64, 64, 64], P('block'), may hold values from -0.75 to 0.75
- value_right: float32 [64, 64, 64], P('block'), may hold values from -0.75 to 0.75
- value_left: float32 [64, 64, 64], P('block'), may hold values from -0.75 to 0.75
- output_right: float32 [64, 64, 64], P('block'), may hold values from -0.75 to 0.75
- output_left: float32 [64, 64, 64], P('block'), may hold values from -0.75 to 0.75
Outputs:
- layer_out: float32 [4096, 2, 1024], P('block', 'groups', ('dp', 'seq')), parts along dimension 1
- grad_inputs: float32 [4096, 2, 1024], P('block', 'groups', ('dp', 'seq')), parts along dimension 1
- grad_seq_right: float32 [16, 128, 128], P(('groups', 'dp', 'seq')), parts along dimension 0
- grad_seq_left: float32 [256, 8, 8], P(('groups', 'dp', 'seq')), parts along dimension 0
- grad_seq_gain: float32 [8192], P(('groups', 'block')), parts along dimension 0
- grad_gate_right: float32 [128, 64, 64], P(('groups', 'block')), parts along dimension 0
- grad_gate_left: float32 [128, 64, 64], P(('groups', 'block')), parts along dimension 0
- grad_value_right: float32 [128, 64, 64], P(('groups', 'block')), parts along dimension 0
- grad_value_left: float32 [128, 64, 64], P(('groups', 'block')), parts along dimension 0
- grad_output_right: float32 [128, 64, 64], P(('groups', 'block')), parts along dimension 0
- grad_output_left: float32 [128, 64, 64], P(('groups', 'block')), parts along dimension 0
The draws below stay inside these ranges and needn't reach their ends.
There are 2 independent parts, one for each index of `groups`. The reference program is written for one: setup_inputs(seed, part) draws one part's arguments, and reference() takes and returns one part's arrays. A program takes and returns all parts, laid end to end along the dimension named above; an argument that names none is the same for every part. Nothing has to cross between parts.
All inputs are finite; a program needn't handle non-finite values.
Results may differ from the reference program's by a relative error of at most 0.00017.
Values sent between devices are 32-bit elements; how exact they have to be, the bound alone decides.
A program may use at most 64 MiB of HBM per device.

```python
import math
import jax
import jax.numpy as jnp
from jax import lax

NB = 64
BS = 64
SB = 128
D = 4096
L = 1024
SN = 8
TOKENS = 1024


def block_levels(key, extent, split, least, high):
    def one(position, blocks):
        draws = jax.random.uniform(jax.random.fold_in(jax.random.fold_in(key, 6), position), (blocks,), jnp.float32, least / len(split), high / len(split))
        return jnp.repeat(jnp.exp(draws), extent[position] // blocks).reshape((-1,) + (1,) * (len(extent) - position - 1))

    level = one(*split[0])
    for cut in split[1:]:
        level = level * one(*cut)
    return level


def gaussian(stream_key, dims, scale, limit, cuts=(), dtype=jnp.bfloat16):
    values = jax.random.normal(stream_key, dims, jnp.float32) * scale
    if len(cuts) > 0:
        values = block_levels(stream_key, dims, cuts, -0.22, 0.18) * values
    return jnp.clip(values, min=-limit, max=limit).astype(dtype)


def setup_inputs(seed: int = 0, part: int = 0) -> dict:
    seeds = jax.random.split(jax.random.key(seed), 12)
    part_keys = jax.random.split(jax.random.fold_in(seeds[11], part), 12)
    return {
        "inputs": gaussian(part_keys[0], (D, 1, L), 1.0, 6.0, ((0, 8), (2, 2)), jnp.float32),
        "cotangent": gaussian(part_keys[1], (D, 1, L), 1.0, 6.0, ((0, 8), (2, 2)), jnp.float32),
        "seq_right": gaussian(seeds[2], (SN, SB, SB), SB ** -0.5, 0.5, ((0, 2),), jnp.float32),
        "seq_left": gaussian(seeds[3], (SB, SN, SN), SN ** -0.5, 2.0, ((0, 2),), jnp.float32),
        "seq_gain": jnp.clip(jnp.exp(math.log(2.0) - 1.3862944 * jax.random.uniform(seeds[4], (D,), jnp.float32) ** block_levels(seeds[4], (D,), ((0, 8),), -0.2, 0.2)), 0.5, 2.0),
        "gate_right": gaussian(seeds[5], (NB, BS, BS), BS ** -0.5, 0.75, ((0, 8),), jnp.float32),
        "gate_left": gaussian(seeds[6], (BS, NB, NB), NB ** -0.5, 0.75, ((0, 8),), jnp.float32),
        "value_right": gaussian(seeds[7], (NB, BS, BS), BS ** -0.5, 0.75, ((0, 8),), jnp.float32),
        "value_left": gaussian(seeds[8], (BS, NB, NB), NB ** -0.5, 0.75, ((0, 8),), jnp.float32),
        "output_right": gaussian(seeds[9], (NB, BS, BS), BS ** -0.5, 0.75, ((0, 8),), jnp.float32),
        "output_left": gaussian(seeds[10], (BS, NB, NB), NB ** -0.5, 0.75, ((0, 8),), jnp.float32),
    }


precise = lax.Precision.HIGHEST

def contract(pattern, former, latter):
    return jnp.einsum(pattern, former, latter, precision=precise)

def monarch(source, factor_right, factor_left):
    blocks = factor_right.shape[0]
    breadth = factor_right.shape[1]
    length = source.shape[1]
    sectioned = contract('bit,bij->bjt', source.reshape(blocks, breadth, length), factor_right)
    turned = contract('bjt,jbk->kjt', sectioned, factor_left)
    return turned.reshape(blocks * breadth, length)

def sequence_mix(source, seq_right, seq_left):
    channels = source.shape[0]
    seq_count = seq_right.shape[0]
    seq_block = seq_right.shape[1]
    sectioned = contract('cai,aij->caj', source.reshape(channels, seq_count, seq_block), seq_right)
    mixed_seq = contract('caj,jab->cbj', sectioned, seq_left)
    return mixed_seq.reshape(channels, seq_count * seq_block)

def gated(gate_in, value_in):
    return jax.nn.gelu(gate_in) * value_in

def mixer_layer(source, seq_right, seq_left, seq_gain, gate_right, gate_left, value_right, value_left, output_right, output_left):
    mixed_in = source + seq_gain[:, None] * sequence_mix(source, seq_right, seq_left)
    hidden = gated(monarch(mixed_in, gate_right, gate_left), monarch(mixed_in, value_right, value_left))
    return mixed_in + monarch(hidden, output_right, output_left)

def reference(inputs, cotangent, seq_right, seq_left, seq_gain, gate_right, gate_left, value_right, value_left, output_right, output_left):
    source = inputs[:, 0, :]
    upstream = cotangent[:, 0, :]
    result, pullback = jax.vjp(mixer_layer, source, seq_right, seq_left, seq_gain, gate_right, gate_left, value_right, value_left, output_right, output_left)
    gradients = pullback(upstream)
    grad_scale = 1.0 / math.sqrt(TOKENS)
    summed = [gradient * grad_scale for gradient in gradients[1:]]
    layer_out = result[:, None, :]
    grad_inputs = gradients[0][:, None, :]
    return (layer_out, grad_inputs, summed[0], summed[1], summed[2], summed[3], summed[4], summed[5], summed[6], summed[7], summed[8])
```

```python
import math

import jax
import jax.numpy as jnp
from jax import lax
from jax.sharding import PartitionSpec as P

LANES = 128
ROWS = ("dp", "seq")
EVERY = ("dp", "seq", "block")


def contract(pattern, former, latter):
    return jnp.einsum(
        pattern, former, latter, precision=lax.Precision.HIGH, preferred_element_type=jnp.float32
    )


def gated(gate_in, value_in):
    return jax.nn.gelu(gate_in) * value_in


def pack(pieces):
    parts, channels, tokens = pieces.shape
    fold = max(1, LANES // tokens)
    folded = pieces.reshape(parts, fold, channels // fold, tokens).transpose(0, 2, 1, 3)
    return folded.reshape(parts, channels // fold, fold * tokens)


def unpack(rows, tokens):
    parts, count, width = rows.shape
    fold = width // tokens
    return rows.reshape(parts, count, fold, tokens).transpose(0, 2, 1, 3).reshape(parts, count * fold, tokens)


def trade(rows, axes):
    return lax.all_to_all(rows, axes, split_axis=0, concat_axis=0, tiled=True)


def body(
    inputs,
    cotangent,
    seq_right,
    seq_left,
    seq_gain,
    gate_right,
    gate_left,
    value_right,
    value_left,
    output_right,
    output_left,
):
    channels = inputs.shape[0]
    length = inputs.shape[1] * inputs.shape[2]
    row_count = lax.axis_size("dp") * lax.axis_size("seq")
    block_count = lax.axis_size("block")
    row_index = lax.axis_index("dp") * lax.axis_size("seq") + lax.axis_index("seq")
    block_index = lax.axis_index("block")
    everyone = row_count * block_count
    source = inputs.reshape(channels, length)
    upstream = cotangent.reshape(channels, length)
    blocks_here = gate_right.shape[0]
    breadth = gate_right.shape[1]
    blocks = blocks_here * block_count
    seq_block = seq_right.shape[1]
    seq_count = seq_right.shape[0] * row_count
    width = blocks * breadth
    mine = channels // row_count
    total = length * row_count
    tokens = length // block_count

    stacked = jnp.concatenate(
        [
            jnp.concatenate([gate_right, value_right], axis=2)[:, None],
            jnp.concatenate([gate_left, value_left], axis=2)[:, None],
            jnp.concatenate([output_right, output_left], axis=2)[:, None],
        ],
        axis=1,
    )
    factors = lax.all_gather(stacked, "block", axis=0, tiled=True)
    right_pair = factors[:, 0]
    gate_l, value_l = factors[:, 1, :, :breadth], factors[:, 1, :, breadth:]
    out_r, out_l = factors[:, 2, :, :breadth], factors[:, 2, :, breadth:]
    right_all = lax.all_gather(seq_right, ROWS, axis=0, tiled=True)
    left_turned = lax.all_gather(seq_left.transpose(1, 2, 0), ROWS, axis=2, tiled=True)

    def to_channels(values):
        arrived = trade(values.reshape(row_count, mine, length), ROWS)
        return arrived.transpose(1, 0, 2).reshape(mine, total)

    own = to_channels(source)
    own_blocks = own.reshape(mine, seq_count, seq_block)
    sectioned_seq = contract("cai,aij->caj", own_blocks, right_all)
    seq_mixed = jnp.sum(left_turned[None] * sectioned_seq[:, :, None, :], axis=1)
    gain = lax.dynamic_slice_in_dim(seq_gain, row_index * mine, mine)
    mixed_own = own + gain[:, None] * seq_mixed.reshape(mine, total)

    def to_tokens(values):
        pieces = values.reshape(mine, everyone, tokens).transpose(1, 0, 2)
        arrived = unpack(trade(pack(pieces), EVERY), tokens)
        return (
            arrived.reshape(row_count, block_count, mine, tokens)
            .transpose(1, 0, 2, 3)
            .reshape(blocks, breadth, tokens)
        )

    across = upstream.reshape(channels, block_count, tokens).transpose(1, 0, 2)
    up = unpack(trade(pack(across), "block"), tokens).reshape(blocks, breadth, tokens)
    mixed = to_tokens(mixed_own)

    pair = contract("bit,bij->bjt", mixed, right_pair)
    gate_s, value_s = pair[:, :breadth], pair[:, breadth:]
    gate_mixed = contract("bjt,jbk->kjt", gate_s, gate_l)
    value_mixed = contract("bjt,jbk->kjt", value_s, value_l)
    hidden, pullback = jax.vjp(gated, gate_mixed, value_mixed)
    output_s = contract("bit,bij->bjt", hidden, out_r)
    layer = mixed + contract("bjt,jbk->kjt", output_s, out_l)

    def to_home(values):
        pieces = values.reshape(block_count, channels, tokens)
        arrived = unpack(trade(pack(pieces), "block"), tokens)
        return arrived.transpose(1, 0, 2).reshape(channels, length)

    layer_out = to_home(layer)

    grad_out_l = contract("bjt,kjt->jbk", output_s, up)
    output_back = contract("jbk,kjt->bjt", out_l, up)
    grad_out_r = contract("bit,bjt->bij", hidden, output_back)
    hidden_back = contract("bij,bjt->bit", out_r, output_back)
    gate_back, value_back = pullback(hidden_back)
    grad_gate_l = contract("bjt,kjt->jbk", gate_s, gate_back)
    grad_value_l = contract("bjt,kjt->jbk", value_s, value_back)
    pair_back = jnp.concatenate(
        [contract("jbk,kjt->bjt", gate_l, gate_back), contract("jbk,kjt->bjt", value_l, value_back)],
        axis=1,
    )
    grad_right_pair = contract("bit,bjt->bij", mixed, pair_back)
    mixed_back = up + contract("bij,bjt->bit", right_pair, pair_back)

    grad_scale = 1.0 / math.sqrt(total)
    grads = jnp.concatenate(
        [
            grad_right_pair[:, None],
            jnp.concatenate([grad_gate_l, grad_value_l], axis=2)[:, None],
            jnp.concatenate([grad_out_r, grad_out_l], axis=2)[:, None],
        ],
        axis=1,
    )
    grads = lax.psum_scatter(grads * grad_scale, "block", scatter_dimension=0, tiled=True)
    grads = lax.psum(grads, ROWS)

    pieces = (
        mixed_back.reshape(block_count, row_count, mine, tokens)
        .transpose(1, 0, 2, 3)
        .reshape(everyone, mine, tokens)
    )
    back_own = unpack(trade(pack(pieces), EVERY), tokens).transpose(1, 0, 2).reshape(mine, total)
    gain_part = jnp.sum(back_own * seq_mixed.reshape(mine, total), axis=1)
    seq_back = (gain[:, None] * back_own).reshape(mine, seq_count, seq_block)
    left_part = jnp.sum(sectioned_seq[:, :, None, :] * seq_back[:, None, :, :], axis=0)
    sectioned_back = jnp.sum(left_turned[None] * seq_back[:, None, :, :], axis=2)
    right_part = contract("cai,caj->aij", own_blocks, sectioned_back)
    grad_own = back_own + contract("aij,caj->cai", right_all, sectioned_back).reshape(mine, total)
    grad_inputs = trade(
        grad_own.reshape(mine, row_count, length).transpose(1, 0, 2), ROWS
    ).reshape(channels, length)

    gain_row = lax.dynamic_update_slice_in_dim(
        jnp.zeros((width,), jnp.float32), gain_part, block_index * channels + row_index * mine, 0
    )
    tail = jnp.concatenate(
        [
            right_part.reshape(-1, LANES),
            left_part.reshape(-1, LANES),
            gain_row.reshape(-1, LANES),
        ],
        axis=0,
    )
    tail = lax.psum(tail * grad_scale, EVERY)
    right_rows = right_part.size // LANES
    left_rows = left_part.size // LANES
    right_sum = lax.dynamic_slice_in_dim(
        tail[:right_rows].reshape(right_part.shape), row_index * seq_right.shape[0], seq_right.shape[0]
    )
    left_sum = lax.dynamic_slice_in_dim(
        tail[right_rows : right_rows + left_rows].reshape(left_part.shape),
        row_index * seq_left.shape[0],
        seq_left.shape[0],
        axis=2,
    ).transpose(2, 0, 1)
    gain_sum = lax.dynamic_slice_in_dim(
        tail[right_rows + left_rows :].reshape(-1), block_index * channels, channels
    )
    return (
        layer_out.reshape(inputs.shape),
        grad_inputs.reshape(inputs.shape),
        right_sum,
        left_sum,
        gain_sum,
        grads[:, 0, :, :breadth],
        grads[:, 1, :, :breadth],
        grads[:, 0, :, breadth:],
        grads[:, 1, :, breadth:],
        grads[:, 2, :, :breadth],
        grads[:, 2, :, breadth:],
    )


def solution(mesh):
    in_specs = (
        P("block", "groups", ("dp", "seq")),
        P("block", "groups", ("dp", "seq")),
        P(("dp", "seq"), None, None),
        P(("dp", "seq"), None, None),
        P("block"),
        P("block", None, None),
        P("block", None, None),
        P("block", None, None),
        P("block", None, None),
        P("block", None, None),
        P("block", None, None),
    )
    out_specs = (
        P("block", "groups", ("dp", "seq")),
        P("block", "groups", ("dp", "seq")),
        P(("groups", "dp", "seq"), None, None),
        P(("groups", "dp", "seq"), None, None),
        P(("groups", "block")),
        P(("groups", "block"), None, None),
        P(("groups", "block"), None, None),
        P(("groups", "block"), None, None),
        P(("groups", "block"), None, None),
        P(("groups", "block"), None, None),
        P(("groups", "block"), None, None),
    )
    return jax.shard_map(body, mesh=mesh, in_specs=in_specs, out_specs=out_specs, check_vma=False)
```

```python
import math

import jax
import jax.numpy as jnp
from jax import lax
from jax.sharding import PartitionSpec as P

LANES = 128
ROWS = ("dp", "seq")
EVERY = ("dp", "seq", "block")


def contract(pattern, former, latter):
    return jnp.einsum(
        pattern, former, latter, precision=lax.Precision.HIGH, preferred_element_type=jnp.float32
    )


def gated(gate_in, value_in):
    return jax.nn.gelu(gate_in) * value_in


def pack(pieces):
    parts, channels, tokens = pieces.shape
    fold = max(1, LANES // tokens)
    folded = pieces.reshape(parts, fold, channels // fold, tokens).transpose(0, 2, 1, 3)
    return folded.reshape(parts, channels // fold, fold * tokens)


def unpack(rows, tokens):
    parts, count, width = rows.shape
    fold = width // tokens
    return rows.reshape(parts, count, fold, tokens).transpose(0, 2, 1, 3).reshape(parts, count * fold, tokens)


def trade(rows, axes):
    return lax.all_to_all(rows, axes, split_axis=0, concat_axis=0, tiled=True)


def body(
    inputs,
    cotangent,
    seq_right,
    seq_left,
    seq_gain,
    gate_right,
    gate_left,
    value_right,
    value_left,
    output_right,
    output_left,
):
    channels = inputs.shape[0]
    length = inputs.shape[1] * inputs.shape[2]
    row_count = lax.axis_size("dp") * lax.axis_size("seq")
    block_count = lax.axis_size("block")
    row_index = lax.axis_index("dp") * lax.axis_size("seq") + lax.axis_index("seq")
    block_index = lax.axis_index("block")
    everyone = row_count * block_count
    source = inputs.reshape(channels, length)
    upstream = cotangent.reshape(channels, length)
    blocks_here = gate_right.shape[0]
    breadth = gate_right.shape[1]
    blocks = blocks_here * block_count
    seq_block = seq_right.shape[1]
    seq_count = seq_right.shape[0] * row_count
    width = blocks * breadth
    mine = channels // row_count
    total = length * row_count
    tokens = length // block_count

    def whole(former, latter):
        return lax.all_gather(jnp.concatenate([former, latter], axis=2), "block", axis=0, tiled=True)

    right_pair = whole(gate_right, value_right)
    left_pair = whole(gate_left, value_left)
    output_pair = whole(output_right, output_left)
    gate_l, value_l = left_pair[:, :, :breadth], left_pair[:, :, breadth:]
    out_r, out_l = output_pair[:, :, :breadth], output_pair[:, :, breadth:]

    def copies(values):
        return jnp.broadcast_to(values[None], (row_count, *values.shape))

    right_rows = copies(seq_right.transpose(1, 0, 2).reshape(seq_block, length))
    left_rows = copies(seq_left.transpose(1, 2, 0).reshape(-1, length))
    arrived = trade(
        jnp.concatenate([source.reshape(row_count, mine, length), right_rows, left_rows], axis=1), ROWS
    )
    own = arrived[:, :mine].transpose(1, 0, 2).reshape(mine, total)
    right_all = (
        arrived[:, mine : mine + seq_block]
        .reshape(row_count, seq_block, seq_right.shape[0], seq_block)
        .transpose(0, 2, 1, 3)
        .reshape(seq_count, seq_block, seq_block)
    )
    left_turned = (
        arrived[:, mine + seq_block :]
        .reshape(row_count, seq_count, seq_count, seq_left.shape[0])
        .transpose(1, 2, 0, 3)
        .reshape(seq_count, seq_count, seq_block)
    )

    own_blocks = own.reshape(mine, seq_count, seq_block)
    sectioned_seq = contract("cai,aij->caj", own_blocks, right_all)
    seq_mixed = jnp.sum(left_turned[None] * sectioned_seq[:, :, None, :], axis=1)
    gain = lax.dynamic_slice_in_dim(seq_gain, row_index * mine, mine)
    mixed_own = own + gain[:, None] * seq_mixed.reshape(mine, total)

    def to_tokens(values):
        pieces = values.reshape(mine, everyone, tokens).transpose(1, 0, 2)
        arrived = unpack(trade(pack(pieces), EVERY), tokens)
        return (
            arrived.reshape(row_count, block_count, mine, tokens)
            .transpose(1, 0, 2, 3)
            .reshape(blocks, breadth, tokens)
        )

    mixed, late = lax.optimization_barrier((to_tokens(mixed_own), upstream))
    across = late.reshape(channels, block_count, tokens).transpose(1, 0, 2)
    up = unpack(trade(pack(across), "block"), tokens).reshape(blocks, breadth, tokens)

    pair = contract("bit,bij->bjt", mixed, right_pair)
    gate_s, value_s = pair[:, :breadth], pair[:, breadth:]
    gate_mixed = contract("bjt,jbk->kjt", gate_s, gate_l)
    value_mixed = contract("bjt,jbk->kjt", value_s, value_l)
    hidden, pullback = jax.vjp(gated, gate_mixed, value_mixed)
    output_s = contract("bit,bij->bjt", hidden, out_r)
    layer = mixed + contract("bjt,jbk->kjt", output_s, out_l)

    leaving, up = lax.optimization_barrier(
        (pack(layer.reshape(block_count, channels, tokens)), up)
    )
    layer_out = unpack(trade(leaving, "block"), tokens).transpose(1, 0, 2).reshape(channels, length)

    grad_scale = 1.0 / math.sqrt(total)

    def summed(former, latter):
        both = jnp.concatenate([former, latter], axis=2) * grad_scale
        part = lax.psum_scatter(both, "block", scatter_dimension=0, tiled=True)
        return part

    grad_out_l = contract("bjt,kjt->jbk", output_s, up)
    output_back = contract("jbk,kjt->bjt", out_l, up)
    grad_out_r = contract("bit,bjt->bij", hidden, output_back)
    output_grads = summed(grad_out_r, grad_out_l)
    hidden_back = contract("bij,bjt->bit", out_r, output_back)
    gate_back, value_back = pullback(hidden_back)
    grad_gate_l = contract("bjt,kjt->jbk", gate_s, gate_back)
    grad_value_l = contract("bjt,kjt->jbk", value_s, value_back)
    left_grads = summed(grad_gate_l, grad_value_l)
    pair_back = jnp.concatenate(
        [contract("jbk,kjt->bjt", gate_l, gate_back), contract("jbk,kjt->bjt", value_l, value_back)],
        axis=1,
    )
    grad_right_pair = contract("bit,bjt->bij", mixed, pair_back)
    mixed_back = up + contract("bij,bjt->bit", right_pair, pair_back)

    right_grads = summed(grad_right_pair[:, :, :breadth], grad_right_pair[:, :, breadth:])

    pieces = (
        mixed_back.reshape(block_count, row_count, mine, tokens)
        .transpose(1, 0, 2, 3)
        .reshape(everyone, mine, tokens)
    )
    back_own = unpack(trade(pack(pieces), EVERY), tokens).transpose(1, 0, 2).reshape(mine, total)
    gain_part = jnp.sum(back_own * seq_mixed.reshape(mine, total), axis=1)
    seq_back = (gain[:, None] * back_own).reshape(mine, seq_count, seq_block)
    left_part = jnp.sum(sectioned_seq[:, :, None, :] * seq_back[:, None, :, :], axis=0)
    sectioned_back = jnp.sum(left_turned[None] * seq_back[:, None, :, :], axis=2)
    right_part = contract("cai,caj->aij", own_blocks, sectioned_back)
    grad_own = back_own + contract("aij,caj->cai", right_all, sectioned_back).reshape(mine, total)
    grad_inputs = trade(
        grad_own.reshape(mine, row_count, length).transpose(1, 0, 2), ROWS
    ).reshape(channels, length)

    gain_row = lax.dynamic_update_slice_in_dim(
        jnp.zeros((width,), jnp.float32), gain_part, block_index * channels + row_index * mine, 0
    )
    right_size = seq_right.size // LANES
    left_size = seq_left.size // LANES
    tail = jnp.concatenate(
        [
            right_part.reshape(row_count, right_size, LANES),
            left_part.reshape(seq_count, seq_count, row_count, seq_left.shape[0])
            .transpose(2, 0, 1, 3)
            .reshape(row_count, left_size, LANES),
            copies(gain_row.reshape(-1, LANES)),
        ],
        axis=1,
    )
    tail_rows = tail.shape[1]
    spare = -tail_rows % block_count
    tail = jnp.pad(tail, ((0, 0), (0, spare), (0, 0)))
    tail = trade(tail.reshape(everyone, -1, LANES), EVERY)
    tail = jnp.sum(tail, axis=0) * grad_scale
    tail = trade(jnp.broadcast_to(tail[None], (block_count, *tail.shape)), "block").reshape(-1, LANES)
    right_sum = tail[:right_size].reshape(seq_right.shape)
    left_sum = (
        tail[right_size : right_size + left_size]
        .reshape(seq_count, seq_count, seq_left.shape[0])
        .transpose(2, 0, 1)
    )
    gain_sum = lax.dynamic_slice_in_dim(
        tail[right_size + left_size : tail_rows].reshape(-1), block_index * channels, channels
    )
    grads = jnp.stack([right_grads, left_grads, output_grads], axis=1)
    if row_count == 2:
        grads = grads + lax.ppermute(grads, ROWS, [(0, 1), (1, 0)])
    else:
        grads = lax.psum(grads, ROWS)
    return (
        layer_out.reshape(inputs.shape),
        grad_inputs.reshape(inputs.shape),
        right_sum,
        left_sum,
        gain_sum,
        grads[:, 0, :, :breadth],
        grads[:, 1, :, :breadth],
        grads[:, 0, :, breadth:],
        grads[:, 1, :, breadth:],
        grads[:, 2, :, :breadth],
        grads[:, 2, :, breadth:],
    )


def solution(mesh):
    in_specs = (
        P("block", "groups", ("dp", "seq")),
        P("block", "groups", ("dp", "seq")),
        P(("dp", "seq"), None, None),
        P(("dp", "seq"), None, None),
        P("block"),
        P("block", None, None),
        P("block", None, None),
        P("block", None, None),
        P("block", None, None),
        P("block", None, None),
        P("block", None, None),
    )
    out_specs = (
        P("block", "groups", ("dp", "seq")),
        P("block", "groups", ("dp", "seq")),
        P(("groups", "dp", "seq"), None, None),
        P(("groups", "dp", "seq"), None, None),
        P(("groups", "block")),
        P(("groups", "block"), None, None),
        P(("groups", "block"), None, None),
        P(("groups", "block"), None, None),
        P(("groups", "block"), None, None),
        P(("groups", "block"), None, None),
        P(("groups", "block"), None, None),
    )
    return jax.shard_map(body, mesh=mesh, in_specs=in_specs, out_specs=out_specs, check_vma=False)
```

```python
import math

import jax
import jax.numpy as jnp
from jax import lax
from jax.sharding import PartitionSpec as P

LANES = 128
ROWS = ("dp", "seq")
EVERY = ("dp", "seq", "block")


def contract(pattern, former, latter):
    return jnp.einsum(
        pattern, former, latter, precision=lax.Precision.HIGH, preferred_element_type=jnp.float32
    )


def gated(gate_in, value_in):
    return jax.nn.gelu(gate_in) * value_in


def pack(pieces):
    parts, channels, tokens = pieces.shape
    fold = max(1, LANES // tokens)
    folded = pieces.reshape(parts, fold, channels // fold, tokens).transpose(0, 2, 1, 3)
    return folded.reshape(parts, channels // fold, fold * tokens)


def unpack(rows, tokens):
    parts, count, width = rows.shape
    fold = width // tokens
    return rows.reshape(parts, count, fold, tokens).transpose(0, 2, 1, 3).reshape(parts, count * fold, tokens)


def trade(rows, axes):
    return lax.all_to_all(rows, axes, split_axis=0, concat_axis=0, tiled=True)


def trade_rows(rows):
    if rows.shape[0] != 2:
        return trade(rows, ROWS)
    me = lax.axis_index("dp") * lax.axis_size("seq") + lax.axis_index("seq")
    kept = lax.dynamic_index_in_dim(rows, me, keepdims=False)
    sent = lax.dynamic_index_in_dim(rows, 1 - me, keepdims=False)
    got = lax.ppermute(sent, ROWS, [(0, 1), (1, 0)])
    first = me == 0
    return jnp.stack([jnp.where(first, kept, got), jnp.where(first, got, kept)])


def body(
    inputs,
    cotangent,
    seq_right,
    seq_left,
    seq_gain,
    gate_right,
    gate_left,
    value_right,
    value_left,
    output_right,
    output_left,
):
    channels = inputs.shape[0]
    length = inputs.shape[1] * inputs.shape[2]
    row_count = lax.axis_size("dp") * lax.axis_size("seq")
    block_count = lax.axis_size("block")
    row_index = lax.axis_index("dp") * lax.axis_size("seq") + lax.axis_index("seq")
    block_index = lax.axis_index("block")
    everyone = row_count * block_count
    source = inputs.reshape(channels, length)
    upstream = cotangent.reshape(channels, length)
    blocks_here = gate_right.shape[0]
    breadth = gate_right.shape[1]
    blocks = blocks_here * block_count
    seq_block = seq_right.shape[1]
    seq_count = seq_right.shape[0] * row_count
    width = blocks * breadth
    mine = channels // row_count
    total = length * row_count
    tokens = length // block_count

    def whole(former, latter):
        return lax.all_gather(jnp.concatenate([former, latter], axis=2), "block", axis=0, tiled=True)

    right_pair = whole(gate_right, value_right)

    def copies(values):
        return jnp.broadcast_to(values[None], (row_count, *values.shape))

    right_rows = copies(seq_right.transpose(1, 0, 2).reshape(seq_block, length))
    left_rows = copies(seq_left.transpose(1, 2, 0).reshape(-1, length))
    arrived = trade_rows(
        jnp.concatenate([source.reshape(row_count, mine, length), right_rows, left_rows], axis=1)
    )
    own = arrived[:, :mine].transpose(1, 0, 2).reshape(mine, total)
    right_all = (
        arrived[:, mine : mine + seq_block]
        .reshape(row_count, seq_block, seq_right.shape[0], seq_block)
        .transpose(0, 2, 1, 3)
        .reshape(seq_count, seq_block, seq_block)
    )
    left_turned = (
        arrived[:, mine + seq_block :]
        .reshape(row_count, seq_count, seq_count, seq_left.shape[0])
        .transpose(1, 2, 0, 3)
        .reshape(seq_count, seq_count, seq_block)
    )

    own_blocks = own.reshape(mine, seq_count, seq_block)
    sectioned_seq = contract("cai,aij->caj", own_blocks, right_all)
    seq_mixed = jnp.sum(left_turned[None] * sectioned_seq[:, :, None, :], axis=1)
    gain = lax.dynamic_slice_in_dim(seq_gain, row_index * mine, mine)
    mixed_own = own + gain[:, None] * seq_mixed.reshape(mine, total)

    leaving = pack(mixed_own.reshape(mine, everyone, tokens).transpose(1, 0, 2))
    across = pack(upstream.reshape(channels, block_count, tokens).transpose(1, 0, 2))
    leaving, across = lax.optimization_barrier((leaving, across))
    tokens_in, across, gate_left, value_left, output_right, output_left = lax.optimization_barrier(
        (trade(leaving, EVERY), across, gate_left, value_left, output_right, output_left)
    )
    left_pair = whole(gate_left, value_left)
    output_pair = whole(output_right, output_left)
    gate_l, value_l = left_pair[:, :, :breadth], left_pair[:, :, breadth:]
    out_r, out_l = output_pair[:, :, :breadth], output_pair[:, :, breadth:]
    mixed = (
        unpack(tokens_in, tokens)
        .reshape(row_count, block_count, mine, tokens)
        .transpose(1, 0, 2, 3)
        .reshape(blocks, breadth, tokens)
    )
    up = unpack(trade(across, "block"), tokens).reshape(blocks, breadth, tokens)

    pair = contract("bit,bij->bjt", mixed, right_pair)
    gate_s, value_s = pair[:, :breadth], pair[:, breadth:]
    gate_mixed = contract("bjt,jbk->kjt", gate_s, gate_l)
    value_mixed = contract("bjt,jbk->kjt", value_s, value_l)
    hidden, pullback = jax.vjp(gated, gate_mixed, value_mixed)
    output_s = contract("bit,bij->bjt", hidden, out_r)
    layer = mixed + contract("bjt,jbk->kjt", output_s, out_l)

    leaving, up = lax.optimization_barrier(
        (pack(layer.reshape(block_count, channels, tokens)), up)
    )
    layer_home = trade(leaving, "block")

    grad_scale = 1.0 / math.sqrt(total)

    def summed(former, latter):
        both = jnp.concatenate([former, latter], axis=2) * grad_scale
        part = lax.psum_scatter(both, "block", scatter_dimension=0, tiled=True)
        if row_count == 2:
            return part + lax.ppermute(part, ROWS, [(0, 1), (1, 0)])
        return lax.psum(part, ROWS)

    grad_out_l = contract("bjt,kjt->jbk", output_s, up)
    output_back = contract("jbk,kjt->bjt", out_l, up)
    grad_out_r = contract("bit,bjt->bij", hidden, output_back)
    output_grads = summed(grad_out_r, grad_out_l)
    hidden_back = contract("bij,bjt->bit", out_r, output_back)
    gate_back, value_back = pullback(hidden_back)
    grad_gate_l = contract("bjt,kjt->jbk", gate_s, gate_back)
    grad_value_l = contract("bjt,kjt->jbk", value_s, value_back)
    left_grads = summed(grad_gate_l, grad_value_l)
    pair_back = jnp.concatenate(
        [contract("jbk,kjt->bjt", gate_l, gate_back), contract("jbk,kjt->bjt", value_l, value_back)],
        axis=1,
    )
    grad_right_pair = contract("bit,bjt->bij", mixed, pair_back)
    mixed_back = up + contract("bij,bjt->bit", right_pair, pair_back)

    right_grads = summed(grad_right_pair[:, :, :breadth], grad_right_pair[:, :, breadth:])

    pieces = (
        mixed_back.reshape(block_count, row_count, mine, tokens)
        .transpose(1, 0, 2, 3)
        .reshape(everyone, mine, tokens)
    )
    returning, layer_home = lax.optimization_barrier((pack(pieces), layer_home))
    back_own = unpack(trade(returning, EVERY), tokens).transpose(1, 0, 2).reshape(mine, total)
    layer_out = unpack(layer_home, tokens).transpose(1, 0, 2).reshape(channels, length)
    gain_part = jnp.sum(back_own * seq_mixed.reshape(mine, total), axis=1)
    seq_back = (gain[:, None] * back_own).reshape(mine, seq_count, seq_block)
    left_part = jnp.sum(sectioned_seq[:, :, None, :] * seq_back[:, None, :, :], axis=0)
    sectioned_back = jnp.sum(left_turned[None] * seq_back[:, None, :, :], axis=2)
    right_part = contract("cai,caj->aij", own_blocks, sectioned_back)
    grad_own = back_own + contract("aij,caj->cai", right_all, sectioned_back).reshape(mine, total)
    grad_inputs = trade_rows(
        grad_own.reshape(mine, row_count, length).transpose(1, 0, 2)
    ).reshape(channels, length)

    gain_row = lax.dynamic_update_slice_in_dim(
        jnp.zeros((width,), jnp.float32), gain_part, block_index * channels + row_index * mine, 0
    )
    right_size = seq_right.size // LANES
    left_size = seq_left.size // LANES
    tail = jnp.concatenate(
        [
            right_part.reshape(row_count, right_size, LANES),
            left_part.reshape(seq_count, seq_count, row_count, seq_left.shape[0])
            .transpose(2, 0, 1, 3)
            .reshape(row_count, left_size, LANES),
            copies(gain_row.reshape(-1, LANES)),
        ],
        axis=1,
    )
    tail_rows = tail.shape[1]
    spare = -tail_rows % block_count
    tail = jnp.pad(tail, ((0, 0), (0, spare), (0, 0)))
    tail = trade(tail.reshape(everyone, -1, LANES), EVERY)
    tail = jnp.sum(tail, axis=0) * grad_scale
    tail = trade(jnp.broadcast_to(tail[None], (block_count, *tail.shape)), "block").reshape(-1, LANES)
    right_sum = tail[:right_size].reshape(seq_right.shape)
    left_sum = (
        tail[right_size : right_size + left_size]
        .reshape(seq_count, seq_count, seq_left.shape[0])
        .transpose(2, 0, 1)
    )
    gain_sum = lax.dynamic_slice_in_dim(
        tail[right_size + left_size : tail_rows].reshape(-1), block_index * channels, channels
    )
    return (
        layer_out.reshape(inputs.shape),
        grad_inputs.reshape(inputs.shape),
        right_sum,
        left_sum,
        gain_sum,
        right_grads[:, :, :breadth],
        left_grads[:, :, :breadth],
        right_grads[:, :, breadth:],
        left_grads[:, :, breadth:],
        output_grads[:, :, :breadth],
        output_grads[:, :, breadth:],
    )


def solution(mesh):
    in_specs = (
        P("block", "groups", ("dp", "seq")),
        P("block", "groups", ("dp", "seq")),
        P(("dp", "seq"), None, None),
        P(("dp", "seq"), None, None),
        P("block"),
        P("block", None, None),
        P("block", None, None),
        P("block", None, None),
        P("block", None, None),
        P("block", None, None),
        P("block", None, None),
    )
    out_specs = (
        P("block", "groups", ("dp", "seq")),
        P("block", "groups", ("dp", "seq")),
        P(("groups", "dp", "seq"), None, None),
        P(("groups", "dp", "seq"), None, None),
        P(("groups", "block")),
        P(("groups", "block"), None, None),
        P(("groups", "block"), None, None),
        P(("groups", "block"), None, None),
        P(("groups", "block"), None, None),
        P(("groups", "block"), None, None),
        P(("groups", "block"), None, None),
    )
    return jax.shard_map(body, mesh=mesh, in_specs=in_specs, out_specs=out_specs, check_vma=False)
```
